512 devices in a mesh: seq: 32 (over z, core), chan: 16 (over y, x).
Axes of the slice: x: 4, y: 4, z: 16, core: 2. Of those that a mesh axis runs over, the one named last changes fastest.
Arguments:
- arrived: bfloat16 [3, 16384, 8192], P(None, ('seq', 'chan')), may hold values from -6 to 6
- landing: int32 [32, 32], P('seq'), may hold values from 0 to 31, each once within a row
- resets: int32 [16384], P('seq'), may hold values 0 or 1
- short_taps: float32 [3, 7, 8192], P(None, None, 'chan'), may hold values from -3 to 3
- decay_rate: float32 [16, 8192], P(None, 'chan'), may hold values from 0 to 1, as said below
- residues: float32 [16, 8192], P(None, 'chan'), may hold values from -2 to 2
- skip_gain: float32 [8192], P('chan'), may hold values from 0.5 to 1.5
Outputs:
- mixed: bfloat16 [16384, 8192], P('seq', 'chan')
The draws below stay inside these ranges and needn't reach their ends.
Inputs may be any that keep to these rules, and one draw needn't show every extreme that they name: Each row is a permutation: landing[r, s] is the place, among the blocks of shard r, of the block that comes from loader group s. `resets`: 1 marks the first token of a document. `decay_rate`: positive decay rates.
All inputs are finite; a program needn't handle non-finite values. No bound on the sum of `resets` on one device may be relied on, other than what follows from the above.
Results may differ from the reference program's by a relative error of at most 0.01.
Values may be sent and summed in bfloat16 or wider, within the bound.
A program may use at most 64 MiB of HBM per device.

```python
import jax
import jax.numpy as jnp
from jax import lax

D = 8192
ORDER = 16
SHORT = 7
TOK_DEV = 512
TOKENS = 16384
SLAB = 16
N_SEQ = 32


def draw_decay_rate(key, part):
    key_spread = jax.random.fold_in(key, 0)
    lowest = jnp.log(jnp.float32(150.0 / (TOKENS * TOKENS)))
    highest = jnp.log(jnp.float32(1.0 / 30.0))
    spread = jax.random.uniform(key_spread, (ORDER, D), jnp.float32)
    log_rates = lowest + spread * (highest - lowest)
    return jnp.exp(log_rates).astype(jnp.float32)


def set_ends(drawn, key, low, largest):
    place = [jax.random.randint(jax.random.fold_in(key, axis), (), 0, length) for axis, length in enumerate(drawn.shape)]
    longest = drawn.shape.index(max(drawn.shape))
    next_to = place[:longest] + [(place[longest] + 1) % drawn.shape[longest]] + place[longest + 1:]
    return drawn.at[tuple(place)].set(low).at[tuple(next_to)].set(largest)


def block_scale(own_key, extent, cuts, least, top_value):
    loudness = 1.0
    for position, shards_of in cuts:
        draws = jax.random.uniform(jax.random.fold_in(jax.random.fold_in(own_key, 6), position), (shards_of,), jnp.float32, least / len(cuts), top_value / len(cuts))
        loudness = loudness * jnp.repeat(jnp.exp(draws), extent[position] // shards_of).reshape((-1,) + (1,) * (len(extent) - 1 - position))
    return loudness


def gaussian(own_key, shape, deviation, reach, cuts=(), kind=jnp.bfloat16):
    result = jax.random.normal(own_key, shape, jnp.float32) * deviation
    if len(cuts) > 0:
        result = block_scale(own_key, shape, cuts, -0.22, 0.18) * result
    return jnp.clip(result, min=-reach, max=reach).astype(kind)


def setup_inputs(seed: int = 0) -> dict:
    key_of = jax.random.split(jax.random.key(seed), 8)
    arrived = gaussian(key_of[0], (3, TOKENS, D), 1.0, 6.0, ((1, 512),))
    landing = jax.vmap(lambda own: jax.random.permutation(own, N_SEQ))(jax.random.split(key_of[1], N_SEQ)).reshape((N_SEQ, N_SEQ)).astype(jnp.int32)
    resets = set_ends((jax.random.randint(key_of[2], (TOKENS,), 0, 8 * TOK_DEV) < 1).astype(jnp.int32), jax.random.fold_in(key_of[2], 1), 0, 1)
    short_taps = gaussian(key_of[3], (3, SHORT, D), 0.5, 3.0, ((2, 16),), jnp.float32)
    decay_rate = draw_decay_rate(jax.random.fold_in(key_of[7], 71), 0)
    residues = gaussian(key_of[5], (ORDER, D), 0.3, 2.0, ((1, 16),), jnp.float32)
    skip_gain = jnp.clip(0.5 + 1.0 * jax.random.uniform(key_of[6], (D,), jnp.float32) ** block_scale(key_of[6], (D,), ((0, 16),), -0.2, 0.2), 0.5, 1.5)
    return dict(arrived=arrived, landing=landing, resets=resets, short_taps=short_taps, decay_rate=decay_rate, residues=residues, skip_gain=skip_gain)


def causal_conv(values, tap_table):
    tap_count = tap_table.shape[0]
    length = values.shape[0]
    padded = jnp.concatenate([jnp.zeros((tap_count - 1, values.shape[1]), values.dtype), values], axis=0)

    def add_tap(tap_index, combined):
        shifted = lax.dynamic_slice_in_dim(padded, tap_count - 1 - tap_index, length, 0)
        return combined + tap_table[tap_index] * shifted
    return lax.fori_loop(0, tap_count, add_tap, jnp.zeros_like(values))

def reference(arrived, landing, resets, short_taps, decay_rate, residues, skip_gain):
    pieces = arrived.reshape(3, N_SEQ, N_SEQ, SLAB, D).transpose(0, 2, 1, 3, 4)
    sources = jnp.argsort(landing, axis=1).astype(jnp.int32)
    row_ids = jnp.arange(N_SEQ, dtype=jnp.int32)[:, None]
    ordered = pieces[:, row_ids, sources].reshape(3, TOKENS, D)
    front_conv = causal_conv(ordered[0].astype(jnp.float32), short_taps[0])
    key_conv = causal_conv(ordered[1].astype(jnp.float32), short_taps[1])
    value_conv = causal_conv(ordered[2].astype(jnp.float32), short_taps[2])
    gated_mix = (key_conv * value_conv).astype(jnp.bfloat16)
    gated_wide = gated_mix.astype(jnp.float32)
    decay_step = jnp.exp(-decay_rate)
    weight = residues * jnp.sqrt(-jnp.expm1(-2.0 * decay_rate))
    keep_mask = (1 - resets).astype(jnp.float32)

    def advance(carried_state, inputs):
        column, hold_flag = inputs
        carried_state = decay_step * carried_state * hold_flag + column[None, :]
        return (carried_state, lax.optimization_barrier(jnp.sum(weight * carried_state, axis=0)))
    _, modal_out = lax.scan(advance, jnp.zeros((ORDER, D), jnp.float32), (gated_wide, keep_mask))
    combined = modal_out + skip_gain[None, :] * gated_wide
    return (front_conv * combined).astype(jnp.bfloat16)
```

```python
import jax
import jax.numpy as jnp
from jax import lax
from jax.experimental import pallas as pl
from jax.experimental.pallas import tpu as pltpu
from jax.sharding import PartitionSpec as P

MESH = pl.DeviceIdType.MESH
ORDERED = (1, 2, 0)
F32 = jnp.float32
BF16 = jnp.bfloat16


def one_minus_exp(u):
    series = jnp.ones_like(u)
    for k in range(10, 1, -1):
        series = 1.0 - (u * (1.0 / k)) * series
    return jnp.where(u < 0.5, u * series, 1.0 - jnp.exp(-u))


def kernel(
    a_ref, land_ref, reset_ref, taps_ref, rate_ref, resid_ref, skip_ref, out_ref,
    mid, buf0, buf1, buf2, hsend, hrecv, ext, gated, modal, res, keep, step_decay, weight, enter, through,
    ends, msg0, sib, l1buf, l2buf, entering, src,
    p1s, p1r, zs, zr, hs, hr, l0s, l0r, l1s, l1r, l2s, l2r,
):
    q = lax.axis_index("seq")
    c = lax.axis_index("chan")
    z = q // 2
    core = q % 2
    group, member = z // 4, z % 4

    def remote(source, target, device, send, recv):
        return pltpu.make_async_remote_copy(
            src_ref=source, dst_ref=target, send_sem=send, recv_sem=recv,
            device_id=device, device_id_type=MESH,
        )

    barrier = pltpu.get_barrier_semaphore()

    @pl.loop(1, 16)
    def _(i):
        pl.semaphore_signal(barrier, inc=1, device_id=(q, lax.rem(c + i, 16)), device_id_type=MESH)

    @pl.loop(1, 32)
    def _(i):
        pl.semaphore_signal(barrier, inc=1, device_id=(lax.rem(q + i, 32), c), device_id_type=MESH)

    pl.semaphore_wait(barrier, 46)

    buf = (buf0, buf1, buf2)

    def columns(dc):
        return pl.ds(pl.multiple_of(dc * 512, 512), 512)

    def shift_at(j):
        return lax.rem(j - 1 + z, 15) + 1

    def plane_send(f, j):
        dc = lax.rem(c + 16 - shift_at(j), 16)
        remote(a_ref.at[f, :, columns(dc)], mid.at[f, j - 1], (q, dc), p1s, p1r.at[f, j - 1]).start()

    def forward(f, block, target_z):
        for k in range(2):
            to = 2 * target_z + k
            rows = block.at[pl.ds(16 * k, 16)]

            @pl.when(to == q)
            def _():
                pltpu.make_async_copy(rows, buf[f].at[q], zr.at[f]).start()

            @pl.when(to != q)
            def _():
                remote(rows, buf[f].at[q], (to, c), zs.at[f], zr.at[f]).start()

    first = ORDERED[0]

    @pl.loop(1, 16)
    def _(j):
        plane_send(first, j)

    @pl.loop(0, 32)
    def _(k):
        total = jnp.int32(0)
        for s in range(32):
            total = jnp.where(land_ref[0, s] == k, jnp.int32(s), total)
        src[k] = total

    for at, f in enumerate(ORDERED):
        if at == 2:
            remote(buf[first].at[pl.ds(0, 31)], buf[first].at[pl.ds(0, 31)], (q, c), zs.at[first], zr.at[first]).wait_send()
        forward(f, a_ref.at[f, :, columns(c)], c)

        @pl.loop(1, 16)
        def _(j, f=f, at=at):
            remote(mid.at[f, j - 1], mid.at[f, j - 1], (q, c), p1s, p1r.at[f, j - 1]).wait_recv()
            forward(f, mid.at[f, j - 1], lax.rem(c + shift_at(j), 16))
            if at < 2:
                plane_send(ORDERED[at + 1], j)

        if at == 0:
            sub = lax.broadcasted_iota(jnp.int32, (8, 128), 0)

            @pl.loop(0, 64)
            def _(t):
                marks = jnp.zeros((8, 128), jnp.int32)
                for i in range(8):
                    marks = jnp.where(sub == i, reset_ref[64 * i + t], marks)
                keep[t] = (1 - marks).astype(F32)

            for l in range(4):
                lanes = pl.ds(128 * l, 128)
                rate = rate_ref[:, lanes]
                decay = jnp.exp(-rate)
                gain = resid_ref[:, lanes] * jnp.sqrt(one_minus_exp(2.0 * rate))
                step_decay[l] = jnp.broadcast_to(decay[:, None, :], (16, 8, 128))
                weight[l] = jnp.broadcast_to(gain[:, None, :], (16, 8, 128))

    sub = lax.broadcasted_iota(jnp.int32, (8, 128), 0)

    def arrived_set(f):
        remote(buf[f], buf[f], (q, c), zs.at[f], zr.at[f]).wait_recv()
        hsend[f] = buf[f][src[31]]
        remote(hsend.at[f], hrecv.at[f], (lax.rem(q + 1, 32), c), hs.at[f], hr.at[f]).start()

        @pl.loop(0, 32)
        def _(k):
            at_row = pl.multiple_of(8 + 16 * k, 8)
            for l in range(4):
                ext[f, l, pl.ds(at_row, 16), :] = buf[f][src[k], :, pl.ds(128 * l, 128)].astype(F32)

    def border(f):
        remote(hsend.at[f], hrecv.at[f], (q, c), hs.at[f], hr.at[f]).wait()
        for l in range(4):
            tail = hrecv[f, :, pl.ds(128 * l, 128)].astype(F32)[8:16]
            ext[f, l, pl.ds(0, 8), :] = jnp.where(q == 0, jnp.zeros_like(tail), tail)

    def conv(f, l, tb):
        first_row = 2 + 8 * tb
        window = jnp.stack([ext[f, l, pl.ds(first_row + m, 8, stride=64), :] for m in range(14)])
        total = taps_ref[f, pl.ds(0, 1), pl.ds(128 * l, 128)][None] * window[6:14]
        for j in range(1, 7):
            total = total + taps_ref[f, pl.ds(j, 1), pl.ds(128 * l, 128)][None] * window[6 - j : 14 - j]
        return total

    def gate(tb):
        for l in range(4):
            product = conv(1, l, tb) * conv(2, l, tb)
            gated[l, pl.ds(8 * tb, 8)] = product.astype(BF16).astype(F32)

    arrived_set(1)
    arrived_set(2)

    @pl.loop(1, 8)
    def _(tb):
        gate(tb)

    border(1)
    border(2)
    gate(0)

    kept = lax.fori_loop(0, 64, lambda t, v: v * keep[t], jnp.ones((8, 128), F32))

    @pl.loop(0, 4)
    def _(l):
        skip = skip_ref[l]

        def advance(t, states):
            value = gated[l, t]
            states = states * (step_decay[l] * keep[t][None]) + value[None]
            modal[l, t] = skip * value + jnp.sum(weight[l] * states, axis=0)
            return states

        states = lax.fori_loop(0, 64, advance, jnp.zeros((16, 8, 128), F32))
        power = step_decay[l]
        for _ in range(6):
            power = power * power
        for n in range(16):
            a, b = power[n] * kept, states[n]
            for by in (1, 2, 4):
                a_before = jnp.where(sub < by, 1.0, pltpu.roll(a, by, 0))
                b_before = jnp.where(sub < by, 0.0, pltpu.roll(b, by, 0))
                b = b + a * b_before
                a = a * a_before
            ends[l, pl.ds(n, 1), :] = b[7:8]
            enter[l, n] = jnp.where(sub < 1, 0.0, pltpu.roll(b, 1, 0))
            through[l, n] = jnp.where(sub < 1, 1.0, pltpu.roll(a, 1, 0))

    unbroken = kept
    for by in (4, 2, 1):
        unbroken = unbroken * pltpu.roll(unbroken, by, 0)
    whole_flag = jnp.concatenate([unbroken, unbroken], axis=0)

    for l in range(4):
        msg0[:, pl.ds(128 * l, 128)] = ends[l].astype(BF16)
    msg0[:, pl.ds(512, 128)] = whole_flag.astype(BF16)
    pair = remote(msg0, sib, (q + 1 - 2 * core, c), l0s, l0r)
    pair.start()
    pair.wait()
    flag_lanes = pl.ds(512, 128)
    own_flag = whole_flag
    sib_flag = sib[:, flag_lanes].astype(F32)
    low = core == 0
    flag0 = jnp.where(low, own_flag, sib_flag)
    flag1 = jnp.where(low, sib_flag, own_flag)

    def rates(l, count):
        return jnp.exp(rate_ref[:, pl.ds(128 * l, 128)] * (-float(count)))

    for l in range(4):
        lanes = pl.ds(128 * l, 128)
        own, other = ends[l], sib[:, lanes].astype(F32)
        end0, end1 = jnp.where(low, own, other), jnp.where(low, other, own)
        l1buf[member, :, lanes] = (end1 + rates(l, 512) * flag1 * end0).astype(BF16)
    l1buf[member, :, flag_lanes] = (flag0 * flag1).astype(BF16)

    for o in range(1, 4):
        to = 2 * (4 * group + lax.rem(member + o, 4)) + core
        remote(l1buf.at[member], l1buf.at[member], (to, c), l1s, l1r).start()
    remote(l1buf.at[pl.ds(0, 3)], l1buf.at[pl.ds(0, 3)], (q, c), l1s, l1r).wait()

    def combine(table, mine, l, count):
        lanes = pl.ds(128 * l, 128)
        power = rates(l, count)
        total = jnp.zeros((16, 128), F32)
        before = jnp.zeros((16, 128), F32)
        passed = jnp.ones((16, 128), F32)
        for i in range(4):
            end = table[i, :, lanes].astype(F32)
            factor = power * table[i, :, flag_lanes].astype(F32)
            earlier = mine > i
            before = jnp.where(earlier, before * factor + end, before)
            passed = jnp.where(earlier, passed * factor, passed)
            total = total * factor + end
        return before, passed, total

    for l in range(4):
        before, passed, total = combine(l1buf, member, l, 1024)
        l2buf[group, :, pl.ds(128 * l, 128)] = total.astype(BF16)
        ends_at = before
        entering[0, l] = ends_at
        entering[1, l] = passed
    flags = l1buf[0, :, flag_lanes] * l1buf[1, :, flag_lanes] * l1buf[2, :, flag_lanes] * l1buf[3, :, flag_lanes]
    l2buf[group, :, flag_lanes] = flags

    for o in range(1, 4):
        to = 2 * (4 * lax.rem(group + o, 4) + member) + core
        remote(l2buf.at[group], l2buf.at[group], (to, c), l2s, l2r).start()
    remote(l2buf.at[pl.ds(0, 3)], l2buf.at[pl.ds(0, 3)], (q, c), l2s, l2r).wait()

    for l in range(4):
        lanes = pl.ds(128 * l, 128)
        before, _, _ = combine(l2buf, group, l, 4096)
        into_chip = entering[0, l] + entering[1, l] * before
        after_core0 = sib[:, lanes].astype(F32) + rates(l, 512) * sib_flag * into_chip
        entering[2, l] = jnp.where(low, into_chip, after_core0)

    @pl.loop(0, 4)
    def _(l):
        into = entering[2, l][:, None, :]
        start = weight[l] * (enter[l] + through[l] * into)

        def carry_on(t, states):
            states = states * (step_decay[l] * keep[t][None])
            modal[l, t] = modal[l, t] + jnp.sum(states, axis=0)
            return states

        lax.fori_loop(0, 64, carry_on, start)

    def finish(tb):
        for l in range(4):
            mixed = conv(0, l, tb) * modal[l, pl.ds(8 * tb, 8)]
            for u in range(8):
                res[l, pl.ds(8 * tb + u, 8, stride=64), :] = mixed[u]

    arrived_set(0)

    @pl.loop(1, 8)
    def _(tb):
        finish(tb)

    border(0)
    finish(0)

    @pl.loop(0, 32)
    def _(k):
        rows = pl.ds(pl.multiple_of(16 * k, 16), 16)
        for l in range(4):
            out_ref[rows, pl.ds(128 * l, 128)] = res[l, rows, :].astype(BF16)

    remote(mid, mid, (q, c), p1s, p1r.at[0, 0]).wait_send()
    for f in (2, 0):
        remote(buf[f].at[pl.ds(0, 31)], buf[f].at[pl.ds(0, 31)], (q, c), zs.at[f], zr.at[f]).wait_send()


def on_device(arrived, landing, resets, short_taps, decay_rate, residues, skip_gain):
    skip = jnp.broadcast_to(skip_gain.reshape(4, 1, 128), (4, 8, 128))
    vmem = pl.BlockSpec(memory_space=pltpu.VMEM)
    smem = pl.BlockSpec(memory_space=pltpu.SMEM)
    dma = pltpu.SemaphoreType.DMA
    return pl.pallas_call(
        kernel,
        out_shape=jax.ShapeDtypeStruct((512, 512), BF16),
        in_specs=[pl.BlockSpec(memory_space=pl.ANY), smem, smem, vmem, vmem, vmem, vmem],
        out_specs=vmem,
        scratch_shapes=[
            pltpu.VMEM((3, 15, 32, 512), BF16),
            pltpu.VMEM((32, 16, 512), BF16),
            pltpu.VMEM((32, 16, 512), BF16),
            pltpu.VMEM((32, 16, 512), BF16),
            pltpu.VMEM((3, 16, 512), BF16),
            pltpu.VMEM((3, 16, 512), BF16),
            pltpu.VMEM((3, 4, 520, 128), F32),
            pltpu.VMEM((4, 64, 8, 128), F32),
            pltpu.VMEM((4, 64, 8, 128), F32),
            pltpu.VMEM((4, 512, 128), F32),
            pltpu.VMEM((64, 8, 128), F32),
            pltpu.VMEM((4, 16, 8, 128), F32),
            pltpu.VMEM((4, 16, 8, 128), F32),
            pltpu.VMEM((4, 16, 8, 128), F32),
            pltpu.VMEM((4, 16, 8, 128), F32),
            pltpu.VMEM((4, 16, 128), F32),
            pltpu.VMEM((16, 640), BF16),
            pltpu.VMEM((16, 640), BF16),
            pltpu.VMEM((4, 16, 640), BF16),
            pltpu.VMEM((4, 16, 640), BF16),
            pltpu.VMEM((3, 4, 16, 128), F32),
            pltpu.SMEM((32,), jnp.int32),
            dma, dma((3, 15)), dma((3,)), dma((3,)), dma((3,)), dma((3,)),
            dma, dma, dma, dma, dma, dma,
        ],
        compiler_params=pltpu.CompilerParams(
            collective_id=0, has_side_effects=True, vmem_limit_bytes=40 << 20
        ),
        cost_estimate=pl.CostEstimate(flops=64 << 20, bytes_accessed=4 << 20, transcendentals=1 << 15),
    )(arrived, landing, resets, short_taps, decay_rate, residues, skip)


def solution(mesh):
    in_specs = (
        P(None, ("seq", "chan"), None),
        P("seq", None),
        P("seq"),
        P(None, None, "chan"),
        P(None, "chan"),
        P(None, "chan"),
        P("chan"),
    )
    return jax.shard_map(
        on_device, mesh=mesh, in_specs=in_specs, out_specs=P("seq", "chan"), check_vma=False
    )
```

```python
import jax
import jax.numpy as jnp
from jax import lax
from jax.experimental import pallas as pl
from jax.experimental.pallas import tpu as pltpu
from jax.sharding import PartitionSpec as P

MESH = pl.DeviceIdType.MESH
HALF = 256
PIECES = ((1, 0), (2, 0), (1, 1), (2, 1), (0, 0), (0, 1))
UNROLL = 4
F32 = jnp.float32
BF16 = jnp.bfloat16


def one_minus_exp(u):
    series = jnp.ones_like(u)
    for k in range(10, 1, -1):
        series = 1.0 - (u * (1.0 / k)) * series
    return jnp.where(u < 0.5, u * series, 1.0 - jnp.exp(-u))


def kernel(
    a_ref, land_ref, reset_ref, taps_ref, rate_ref, resid_ref, skip_ref, out_ref,
    mid, buf0, buf1, buf2, buf3, buf4, buf5, hsend, hrecv, ext, gated, modal, res, keep, step_decay, weight, enter, through,
    ends, msg0, sib, l1buf, l2buf, entering, src,
    p1s, p1r, zs, zr, hs, hr, l0s, l0r, l1s, l1r, l2s, l2r, far,
):
    q = lax.axis_index("seq")
    c = lax.axis_index("chan")
    z = q // 2
    core = q % 2
    group, member = z // 4, z % 4

    def remote(source, target, device, send, recv):
        return pltpu.make_async_remote_copy(
            src_ref=source, dst_ref=target, send_sem=send, recv_sem=recv,
            device_id=device, device_id_type=MESH,
        )

    barrier = pltpu.get_barrier_semaphore()

    def greet(device):
        pl.semaphore_signal(barrier, inc=1, device_id=device, device_id_type=MESH)

    @pl.loop(1, 16)
    def _(i):
        greet((q, lax.rem(c + i, 16)))

    @pl.loop(1, 5)
    def _(i):
        for k in range(2):
            greet((2 * lax.rem(z + i, 16) + k, c))
            greet((2 * lax.rem(z + 16 - i, 16) + k, c))

    greet((q + 1 - 2 * core, c))
    pl.semaphore_wait(barrier, 32)
    for beyond in (8, 24):
        pl.semaphore_signal(far, inc=1, device_id=(lax.rem(q + beyond, 32), c), device_id_type=MESH)

    buf = (buf0, buf1, buf2, buf3, buf4, buf5)

    def columns(dc, half):
        return pl.ds(pl.multiple_of(dc * 512 + half * HALF, 128), HALF)

    def shift_at(j):
        return lax.rem(j - 1 + z, 15) + 1

    def plane_send(p, j):
        f, half = PIECES[p]
        dc = lax.rem(c + 16 - shift_at(j), 16)
        remote(a_ref.at[f, :, columns(dc, half)], mid.at[p, j - 1], (q, dc), p1s, p1r.at[p, j - 1]).start()

    def ring_send(p, block, target_z):
        for k in range(2):
            to = 2 * target_z + k
            rows = block.at[pl.ds(16 * k, 16)]

            @pl.when(to == q)
            def _():
                pltpu.make_async_copy(rows, buf[p].at[q], zr.at[p]).start()

            @pl.when(to != q)
            def _():
                remote(rows, buf[p].at[q], (to, c), zs.at[p], zr.at[p]).start()

    def forward(p, first=0, stop=16):
        f, half = PIECES[p]
        if first == 0:
            ring_send(p, a_ref.at[f, :, columns(c, half)], c)

        @pl.loop(max(first, 1), stop)
        def _(j):
            remote(mid.at[p, j - 1], mid.at[p, j - 1], (q, c), p1s, p1r.at[p, j - 1]).wait_recv()
            ring_send(p, mid.at[p, j - 1], lax.rem(c + shift_at(j), 16))
            if p + 1 < len(PIECES):
                plane_send(p + 1, j)

    @pl.loop(1, 16)
    def _(j):
        plane_send(0, j)

    @pl.loop(0, 32)
    def _(k):
        total = jnp.int32(0)
        for s in range(32):
            total = jnp.where(land_ref[0, s] == k, jnp.int32(s), total)
        src[k] = total

    pl.semaphore_wait(far, 2)
    forward(0)

    sub = lax.broadcasted_iota(jnp.int32, (8, 128), 0)

    @pl.loop(0, 64)
    def _(t):
        marks = jnp.zeros((8, 128), jnp.int32)
        for i in range(8):
            marks = jnp.where(sub == i, reset_ref[64 * i + t], marks)
        keep[t] = (1 - marks).astype(F32)

    for l in range(4):
        lanes = pl.ds(128 * l, 128)
        rate = rate_ref[:, lanes]
        decay = jnp.exp(-rate)
        gain = resid_ref[:, lanes] * jnp.sqrt(one_minus_exp(2.0 * rate))
        step_decay[l] = jnp.broadcast_to(decay[:, None, :], (16, 8, 128))
        weight[l] = jnp.broadcast_to(gain[:, None, :], (16, 8, 128))

    kept = lax.fori_loop(0, 64, lambda t, v: v * keep[t], jnp.ones((8, 128), F32))

    for p in (1, 2, 3):
        forward(p)

    def sum16(v):
        v = v[:8] + v[8:]
        v = v[:4] + v[4:]
        v = v[:2] + v[2:]
        return v[0] + v[1]

    def arrived_piece(p):
        f, half = PIECES[p]
        remote(buf[p], buf[p], (q, c), zs.at[p], zr.at[p]).wait_recv()
        hsend[p] = buf[p][src[31]]
        remote(hsend.at[p], hrecv.at[p], (lax.rem(q + 1, 32), c), hs.at[p], hr.at[p]).start()

        @pl.loop(0, 32)
        def _(k):
            at_row = pl.multiple_of(8 + 16 * k, 8)
            for i in range(2):
                ext[f, 2 * half + i, pl.ds(at_row, 16), :] = buf[p][src[k], :, pl.ds(128 * i, 128)].astype(F32)

    def border(p):
        f, half = PIECES[p]
        remote(hsend.at[p], hrecv.at[p], (q, c), hs.at[p], hr.at[p]).wait()
        for i in range(2):
            tail = hrecv[p, :, pl.ds(128 * i, 128)].astype(F32)[8:16]
            ext[f, 2 * half + i, pl.ds(0, 8), :] = jnp.where(q == 0, jnp.zeros_like(tail), tail)

    def conv(f, l, tb):
        first_row = 2 + 8 * tb
        window = jnp.stack([ext[f, l, pl.ds(first_row + m, 8, stride=64), :] for m in range(14)])
        total = taps_ref[f, pl.ds(0, 1), pl.ds(128 * l, 128)][None] * window[6:14]
        for j in range(1, 7):
            total = total + taps_ref[f, pl.ds(j, 1), pl.ds(128 * l, 128)][None] * window[6 - j : 14 - j]
        return total

    def gate(l, tb):
        product = conv(1, l, tb) * conv(2, l, tb)
        gated[l, pl.ds(8 * tb, 8)] = product.astype(BF16).astype(F32)

    def scan_lanes(l):
        skip = skip_ref[l]

        def advance(step, states):
            for u in range(UNROLL):
                t = UNROLL * step + u
                value = gated[l, t]
                states = states * (step_decay[l] * keep[t][None]) + value[None]
                modal[l, t] = skip * value + sum16(weight[l] * states)
            return states

        states = lax.fori_loop(0, 64 // UNROLL, advance, jnp.zeros((16, 8, 128), F32))
        power = step_decay[l]
        for _ in range(6):
            power = power * power
        for n in range(16):
            a, b = power[n] * kept, states[n]
            for by in (1, 2, 4):
                a_before = jnp.where(sub < by, 1.0, pltpu.roll(a, by, 0))
                b_before = jnp.where(sub < by, 0.0, pltpu.roll(b, by, 0))
                b = b + a * b_before
                a = a * a_before
            ends[l, pl.ds(n, 1), :] = b[7:8]
            enter[l, n] = jnp.where(sub < 1, 0.0, pltpu.roll(b, 1, 0))
            through[l, n] = jnp.where(sub < 1, 1.0, pltpu.roll(a, 1, 0))

    def gate_and_scan(half):
        lanes = (2 * half, 2 * half + 1)

        @pl.loop(1, 8)
        def _(tb):
            for l in lanes:
                gate(l, tb)

        border(2 * half)
        border(2 * half + 1)
        for l in lanes:
            gate(l, 0)
        pl.loop(lanes[0], lanes[1] + 1)(scan_lanes)

    arrived_piece(0)
    arrived_piece(1)
    gate_and_scan(0)
    forward(4, 0, 6)
    arrived_piece(2)
    arrived_piece(3)
    forward(4, 6, 14)
    gate_and_scan(1)

    unbroken = kept
    for by in (4, 2, 1):
        unbroken = unbroken * pltpu.roll(unbroken, by, 0)
    whole_flag = jnp.concatenate([unbroken, unbroken], axis=0)

    for l in range(4):
        msg0[:, pl.ds(128 * l, 128)] = ends[l].astype(BF16)
    msg0[:, pl.ds(512, 128)] = whole_flag.astype(BF16)
    pair = remote(msg0, sib, (q + 1 - 2 * core, c), l0s, l0r)
    pair.start()
    forward(4, 14, 16)
    pair.wait()
    flag_lanes = pl.ds(512, 128)
    own_flag = whole_flag
    sib_flag = sib[:, flag_lanes].astype(F32)
    low = core == 0
    flag0 = jnp.where(low, own_flag, sib_flag)
    flag1 = jnp.where(low, sib_flag, own_flag)

    def rates(l, count):
        return jnp.exp(rate_ref[:, pl.ds(128 * l, 128)] * (-float(count)))

    for l in range(4):
        lanes = pl.ds(128 * l, 128)
        own, other = ends[l], sib[:, lanes].astype(F32)
        end0, end1 = jnp.where(low, own, other), jnp.where(low, other, own)
        l1buf[member, :, lanes] = (end1 + rates(l, 512) * flag1 * end0).astype(BF16)
    l1buf[member, :, flag_lanes] = (flag0 * flag1).astype(BF16)

    for o in range(1, 4):
        to = 2 * (4 * group + lax.rem(member + o, 4)) + core
        remote(l1buf.at[member], l1buf.at[member], (to, c), l1s, l1r).start()
    forward(5, 0, 8)
    remote(l1buf.at[pl.ds(0, 3)], l1buf.at[pl.ds(0, 3)], (q, c), l1s, l1r).wait()

    def combine(table, mine, l, count):
        lanes = pl.ds(128 * l, 128)
        power = rates(l, count)
        total = jnp.zeros((16, 128), F32)
        before = jnp.zeros((16, 128), F32)
        passed = jnp.ones((16, 128), F32)
        for i in range(4):
            end = table[i, :, lanes].astype(F32)
            factor = power * table[i, :, flag_lanes].astype(F32)
            earlier = mine > i
            before = jnp.where(earlier, before * factor + end, before)
            passed = jnp.where(earlier, passed * factor, passed)
            total = total * factor + end
        return before, passed, total

    for l in range(4):
        before, passed, total = combine(l1buf, member, l, 1024)
        l2buf[group, :, pl.ds(128 * l, 128)] = total.astype(BF16)
        ends_at = before
        entering[0, l] = ends_at
        entering[1, l] = passed
    flags = l1buf[0, :, flag_lanes] * l1buf[1, :, flag_lanes] * l1buf[2, :, flag_lanes] * l1buf[3, :, flag_lanes]
    l2buf[group, :, flag_lanes] = flags

    for o in range(1, 4):
        to = 2 * (4 * lax.rem(group + o, 4) + member) + core
        remote(l2buf.at[group], l2buf.at[group], (to, c), l2s, l2r).start()
    forward(5, 8, 16)
    remote(l2buf.at[pl.ds(0, 3)], l2buf.at[pl.ds(0, 3)], (q, c), l2s, l2r).wait()

    for l in range(4):
        lanes = pl.ds(128 * l, 128)
        before, _, _ = combine(l2buf, group, l, 4096)
        into_chip = entering[0, l] + entering[1, l] * before
        after_core0 = sib[:, lanes].astype(F32) + rates(l, 512) * sib_flag * into_chip
        entering[2, l] = jnp.where(low, into_chip, after_core0)

    @pl.loop(0, 4)
    def _(l):
        into = entering[2, l][:, None, :]
        start = weight[l] * (enter[l] + through[l] * into)

        def carry_on(step, carried):
            states, held = carried
            for u in range(UNROLL):
                t = UNROLL * step + u
                held = held * keep[t]
                states = states * step_decay[l]
                modal[l, t] = modal[l, t] + held * sum16(states)
            return states, held

        lax.fori_loop(0, 64 // UNROLL, carry_on, (start, jnp.ones((8, 128), F32)))

    def finish(l, tb):
        mixed = conv(0, l, tb) * modal[l, pl.ds(8 * tb, 8)]
        for u in range(8):
            res[l, pl.ds(8 * tb + u, 8, stride=64), :] = mixed[u]

    for half in range(2):
        lanes = (2 * half, 2 * half + 1)
        arrived_piece(4 + half)

        @pl.loop(1, 8)
        def _(tb):
            for l in lanes:
                finish(l, tb)

        border(4 + half)
        for l in lanes:
            finish(l, 0)

        @pl.loop(0, 32)
        def _(k):
            rows = pl.ds(pl.multiple_of(16 * k, 16), 16)
            for l in lanes:
                out_ref[rows, pl.ds(128 * l, 128)] = res[l, rows, :].astype(BF16)

    remote(mid, mid, (q, c), p1s, p1r.at[0, 0]).wait_send()
    for p in range(len(PIECES)):
        gone = buf[p].at[pl.ds(0, 31)]
        remote(gone, gone, (q, c), zs.at[p], zr.at[p]).wait_send()


def on_device(arrived, landing, resets, short_taps, decay_rate, residues, skip_gain):
    skip = jnp.broadcast_to(skip_gain.reshape(4, 1, 128), (4, 8, 128))
    vmem = pl.BlockSpec(memory_space=pltpu.VMEM)
    smem = pl.BlockSpec(memory_space=pltpu.SMEM)
    dma = pltpu.SemaphoreType.DMA
    return pl.pallas_call(
        kernel,
        out_shape=jax.ShapeDtypeStruct((512, 512), BF16),
        in_specs=[pl.BlockSpec(memory_space=pl.ANY), smem, smem, vmem, vmem, vmem, vmem],
        out_specs=vmem,
        scratch_shapes=[
            pltpu.VMEM((6, 15, 32, HALF), BF16),
            *[pltpu.VMEM((32, 16, HALF), BF16)] * 6,
            pltpu.VMEM((6, 16, HALF), BF16),
            pltpu.VMEM((6, 16, HALF), BF16),
            pltpu.VMEM((3, 4, 520, 128), F32),
            pltpu.VMEM((4, 64, 8, 128), F32),
            pltpu.VMEM((4, 64, 8, 128), F32),
            pltpu.VMEM((4, 512, 128), F32),
            pltpu.VMEM((64, 8, 128), F32),
            pltpu.VMEM((4, 16, 8, 128), F32),
            pltpu.VMEM((4, 16, 8, 128), F32),
            pltpu.VMEM((4, 16, 8, 128), F32),
            pltpu.VMEM((4, 16, 8, 128), F32),
            pltpu.VMEM((4, 16, 128), F32),
            pltpu.VMEM((16, 640), BF16),
            pltpu.VMEM((16, 640), BF16),
            pltpu.VMEM((4, 16, 640), BF16),
            pltpu.VMEM((4, 16, 640), BF16),
            pltpu.VMEM((3, 4, 16, 128), F32),
            pltpu.SMEM((32,), jnp.int32),
            dma, dma((6, 15)), dma((6,)), dma((6,)), dma((6,)), dma((6,)),
            dma, dma, dma, dma, dma, dma, pltpu.SemaphoreType.REGULAR,
        ],
        compiler_params=pltpu.CompilerParams(
            collective_id=0, has_side_effects=True, vmem_limit_bytes=40 << 20
        ),
        cost_estimate=pl.CostEstimate(flops=64 << 20, bytes_accessed=4 << 20, transcendentals=1 << 15),
    )(arrived, landing, resets, short_taps, decay_rate, residues, skip)


def solution(mesh):
    in_specs = (
        P(None, ("seq", "chan"), None),
        P("seq", None),
        P("seq"),
        P(None, None, "chan"),
        P(None, "chan"),
        P(None, "chan"),
        P("chan"),
    )
    return jax.shard_map(
        on_device, mesh=mesh, in_specs=in_specs, out_specs=P("seq", "chan"), check_vma=False
    )
```

```python
import jax
import jax.numpy as jnp
from jax import lax
from jax.experimental import pallas as pl
from jax.experimental.pallas import tpu as pltpu
from jax.sharding import PartitionSpec as P

MESH = pl.DeviceIdType.MESH
PARTS = ((0, 2), (2, 2))
PIECES = ((1, 0), (2, 0), (1, 1), (2, 1), (0, 0), (0, 1))
UNROLL = 8
F32 = jnp.float32
BF16 = jnp.bfloat16


def one_minus_exp(u):
    series = jnp.ones_like(u)
    for k in range(10, 1, -1):
        series = 1.0 - (u * (1.0 / k)) * series
    return jnp.where(u < 0.5, u * series, 1.0 - jnp.exp(-u))


def kernel(
    a_ref, land_ref, reset_ref, taps_ref, rate_ref, resid_ref, skip_ref, out_ref,
    mid0, mid1, mid2, mid3, mid4, mid5, buf0, buf1, buf2, buf3, buf4, buf5,
    hsend0, hsend1, hsend2, hsend3, hsend4, hsend5, hrecv0, hrecv1, hrecv2, hrecv3, hrecv4, hrecv5, ext, gated, modal, res, keep, step_decay, weight, enter, through,
    ends, msg0, sib, l1buf, l2buf, entering, src,
    p1s, p1r, zs, zr, hs, hr, l0s, l0r, l1s, l1r, l2s, l2r, far,
):
    q = lax.axis_index("seq")
    c = lax.axis_index("chan")
    z = q // 2
    core = q % 2
    group, member = z // 4, z % 4

    def remote(source, target, device, send, recv):
        return pltpu.make_async_remote_copy(
            src_ref=source, dst_ref=target, send_sem=send, recv_sem=recv,
            device_id=device, device_id_type=MESH,
        )

    barrier = pltpu.get_barrier_semaphore()

    def greet(device):
        pl.semaphore_signal(barrier, inc=1, device_id=device, device_id_type=MESH)

    @pl.loop(1, 16)
    def _(i):
        greet((q, lax.rem(c + i, 16)))

    @pl.loop(1, 5)
    def _(i):
        for k in range(2):
            greet((2 * lax.rem(z + i, 16) + k, c))
            greet((2 * lax.rem(z + 16 - i, 16) + k, c))

    greet((q + 1 - 2 * core, c))
    pl.semaphore_wait(barrier, 32)
    for beyond in (8, 24):
        pl.semaphore_signal(far, inc=1, device_id=(lax.rem(q + beyond, 32), c), device_id_type=MESH)

    mid = (mid0, mid1, mid2, mid3, mid4, mid5)
    buf = (buf0, buf1, buf2, buf3, buf4, buf5)
    hsend = (hsend0, hsend1, hsend2, hsend3, hsend4, hsend5)
    hrecv = (hrecv0, hrecv1, hrecv2, hrecv3, hrecv4, hrecv5)

    def columns(dc, half):
        group0, groups = PARTS[half]
        return pl.ds(pl.multiple_of(dc * 512 + 128 * group0, 128), 128 * groups)

    def shift_at(j):
        return lax.rem(j - 1 + z, 15) + 1

    def plane_send(p, j):
        f, half = PIECES[p]
        dc = lax.rem(c + 16 - shift_at(j), 16)
        remote(a_ref.at[f, :, columns(dc, half)], mid[p].at[j - 1], (q, dc), p1s.at[p], p1r.at[p, j - 1]).start()

    def ring_send(p, block, target_z):
        for k in range(2):
            to = 2 * target_z + k
            rows = block.at[pl.ds(16 * k, 16)]

            @pl.when(to == q)
            def _():
                pltpu.make_async_copy(rows, buf[p].at[q], zr.at[p]).start()

            @pl.when(to != q)
            def _():
                remote(rows, buf[p].at[q], (to, c), zs.at[p], zr.at[p]).start()

    def forward(p, first=0, stop=16):
        f, half = PIECES[p]
        if first == 0:
            ring_send(p, a_ref.at[f, :, columns(c, half)], c)

        @pl.loop(max(first, 1), stop)
        def _(j):
            remote(mid[p].at[j - 1], mid[p].at[j - 1], (q, c), p1s.at[p], p1r.at[p, j - 1]).wait_recv()
            ring_send(p, mid[p].at[j - 1], lax.rem(c + shift_at(j), 16))
            for ahead in ((p + 1,) if p < 3 else (4, 5) if p == 3 else ()):
                plane_send(ahead, j)

    @pl.loop(1, 16)
    def _(j):
        plane_send(0, j)

    @pl.loop(0, 32)
    def _(k):
        total = jnp.int32(0)
        for s in range(32):
            total = jnp.where(land_ref[0, s] == k, jnp.int32(s), total)
        src[k] = total

    pl.semaphore_wait(far, 2)
    forward(0)

    sub = lax.broadcasted_iota(jnp.int32, (8, 128), 0)

    @pl.loop(0, 64)
    def _(t):
        marks = jnp.zeros((8, 128), jnp.int32)
        for i in range(8):
            marks = jnp.where(sub == i, reset_ref[64 * i + t], marks)
        keep[t] = (1 - marks).astype(F32)

    for l in range(4):
        lanes = pl.ds(128 * l, 128)
        rate = rate_ref[:, lanes]
        decay = jnp.exp(-rate)
        gain = resid_ref[:, lanes] * jnp.sqrt(one_minus_exp(2.0 * rate))
        step_decay[l] = jnp.broadcast_to(decay[:, None, :], (16, 8, 128))
        weight[l] = jnp.broadcast_to(gain[:, None, :], (16, 8, 128))

    kept = lax.fori_loop(0, 64, lambda t, v: v * keep[t], jnp.ones((8, 128), F32))

    for p in (1, 2, 3):
        forward(p)

    def sum16(v):
        v = v[:8] + v[8:]
        v = v[:4] + v[4:]
        v = v[:2] + v[2:]
        return v[0] + v[1]

    def arrived_piece(p):
        f, half = PIECES[p]
        remote(buf[p], buf[p], (q, c), zs.at[p], zr.at[p]).wait_recv()
        hsend[p][...] = buf[p][src[31]]
        remote(hsend[p], hrecv[p], (lax.rem(q + 1, 32), c), hs.at[p], hr.at[p]).start()

        @pl.loop(0, 32)
        def _(k):
            at_row = pl.multiple_of(8 + 16 * k, 8)
            for i in range(PARTS[half][1]):
                ext[f, PARTS[half][0] + i, pl.ds(at_row, 16), :] = buf[p][src[k], :, pl.ds(128 * i, 128)].astype(F32)

    def border(p):
        f, half = PIECES[p]
        remote(hsend[p], hrecv[p], (q, c), hs.at[p], hr.at[p]).wait()
        for i in range(PARTS[half][1]):
            tail = hrecv[p][:, pl.ds(128 * i, 128)].astype(F32)[8:16]
            ext[f, PARTS[half][0] + i, pl.ds(0, 8), :] = jnp.where(q == 0, jnp.zeros_like(tail), tail)

    def conv(f, l, tb):
        first_row = 2 + 8 * tb
        window = jnp.stack([ext[f, l, pl.ds(first_row + m, 8, stride=64), :] for m in range(14)])
        total = taps_ref[f, pl.ds(0, 1), pl.ds(128 * l, 128)][None] * window[6:14]
        for j in range(1, 7):
            total = total + taps_ref[f, pl.ds(j, 1), pl.ds(128 * l, 128)][None] * window[6 - j : 14 - j]
        return total

    def gate(l, tb):
        product = conv(1, l, tb) * conv(2, l, tb)
        gated[l, pl.ds(8 * tb, 8)] = product.astype(BF16).astype(F32)

    def scan_lanes(l):
        skip = skip_ref[l]

        def advance(step, states):
            for u in range(UNROLL):
                t = UNROLL * step + u
                value = gated[l, t]
                states = states * (step_decay[l] * keep[t][None]) + value[None]
                modal[l, t] = skip * value + sum16(weight[l] * states)
            return states

        states = lax.fori_loop(0, 64 // UNROLL, advance, jnp.zeros((16, 8, 128), F32))
        power = step_decay[l]
        for _ in range(6):
            power = power * power
        for n in range(16):
            a, b = power[n] * kept, states[n]
            for by in (1, 2, 4):
                a_before = jnp.where(sub < by, 1.0, pltpu.roll(a, by, 0))
                b_before = jnp.where(sub < by, 0.0, pltpu.roll(b, by, 0))
                b = b + a * b_before
                a = a * a_before
            ends[l, pl.ds(n, 1), :] = b[7:8]
            enter[l, n] = jnp.where(sub < 1, 0.0, pltpu.roll(b, 1, 0))
            through[l, n] = jnp.where(sub < 1, 1.0, pltpu.roll(a, 1, 0))

    def gate_and_scan(half):
        lanes = tuple(range(PARTS[half][0], sum(PARTS[half])))

        @pl.loop(1, 8)
        def _(tb):
            for l in lanes:
                gate(l, tb)

        border(2 * half)
        border(2 * half + 1)
        for l in lanes:
            gate(l, 0)
        pl.loop(lanes[0], lanes[-1] + 1)(scan_lanes)

    arrived_piece(0)
    arrived_piece(1)
    gate_and_scan(0)
    forward(4, 0, 6)
    arrived_piece(2)
    arrived_piece(3)
    forward(4, 6, 16)
    gate_and_scan(1)

    unbroken = kept
    for by in (4, 2, 1):
        unbroken = unbroken * pltpu.roll(unbroken, by, 0)
    whole_flag = jnp.concatenate([unbroken, unbroken], axis=0)

    for l in range(4):
        msg0[:, pl.ds(128 * l, 128)] = ends[l].astype(BF16)
    msg0[:, pl.ds(512, 128)] = whole_flag.astype(BF16)
    pair = remote(msg0, sib, (q + 1 - 2 * core, c), l0s, l0r)
    pair.start()
    pair.wait()
    flag_lanes = pl.ds(512, 128)
    own_flag = whole_flag
    sib_flag = sib[:, flag_lanes].astype(F32)
    low = core == 0
    flag0 = jnp.where(low, own_flag, sib_flag)
    flag1 = jnp.where(low, sib_flag, own_flag)

    def rates(l, count):
        return jnp.exp(rate_ref[:, pl.ds(128 * l, 128)] * (-float(count)))

    for l in range(4):
        lanes = pl.ds(128 * l, 128)
        own, other = ends[l], sib[:, lanes].astype(F32)
        end0, end1 = jnp.where(low, own, other), jnp.where(low, other, own)
        l1buf[member, :, lanes] = (end1 + rates(l, 512) * flag1 * end0).astype(BF16)
    l1buf[member, :, flag_lanes] = (flag0 * flag1).astype(BF16)

    for o in range(1, 4):
        to = 2 * (4 * group + lax.rem(member + o, 4)) + core
        remote(l1buf.at[member], l1buf.at[member], (to, c), l1s, l1r).start()
    forward(5, 0, 10)
    remote(l1buf.at[pl.ds(0, 3)], l1buf.at[pl.ds(0, 3)], (q, c), l1s, l1r).wait()

    def combine(table, mine, l, count):
        lanes = pl.ds(128 * l, 128)
        power = rates(l, count)
        total = jnp.zeros((16, 128), F32)
        before = jnp.zeros((16, 128), F32)
        passed = jnp.ones((16, 128), F32)
        for i in range(4):
            end = table[i, :, lanes].astype(F32)
            factor = power * table[i, :, flag_lanes].astype(F32)
            earlier = mine > i
            before = jnp.where(earlier, before * factor + end, before)
            passed = jnp.where(earlier, passed * factor, passed)
            total = total * factor + end
        return before, passed, total

    for l in range(4):
        before, passed, total = combine(l1buf, member, l, 1024)
        l2buf[group, :, pl.ds(128 * l, 128)] = total.astype(BF16)
        ends_at = before
        entering[0, l] = ends_at
        entering[1, l] = passed
    flags = l1buf[0, :, flag_lanes] * l1buf[1, :, flag_lanes] * l1buf[2, :, flag_lanes] * l1buf[3, :, flag_lanes]
    l2buf[group, :, flag_lanes] = flags

    for o in range(1, 4):
        to = 2 * (4 * lax.rem(group + o, 4) + member) + core
        remote(l2buf.at[group], l2buf.at[group], (to, c), l2s, l2r).start()
    forward(5, 10, 16)
    remote(l2buf.at[pl.ds(0, 3)], l2buf.at[pl.ds(0, 3)], (q, c), l2s, l2r).wait()

    for l in range(4):
        lanes = pl.ds(128 * l, 128)
        before, _, _ = combine(l2buf, group, l, 4096)
        into_chip = entering[0, l] + entering[1, l] * before
        after_core0 = sib[:, lanes].astype(F32) + rates(l, 512) * sib_flag * into_chip
        entering[2, l] = jnp.where(low, into_chip, after_core0)

    @pl.loop(0, 4)
    def _(l):
        into = entering[2, l][:, None, :]
        start = weight[l] * (enter[l] + through[l] * into)

        def carry_on(step, carried):
            states, held = carried
            for u in range(UNROLL):
                t = UNROLL * step + u
                held = held * keep[t]
                states = states * step_decay[l]
                modal[l, t] = modal[l, t] + held * sum16(states)
            return states, held

        lax.fori_loop(0, 64 // UNROLL, carry_on, (start, jnp.ones((8, 128), F32)))

    def finish(l, tb):
        mixed = conv(0, l, tb) * modal[l, pl.ds(8 * tb, 8)]
        for u in range(8):
            res[l, pl.ds(8 * tb + u, 8, stride=64), :] = mixed[u]

    for half in range(2):
        lanes = tuple(range(PARTS[half][0], sum(PARTS[half])))
        arrived_piece(4 + half)

        @pl.loop(1, 8)
        def _(tb):
            for l in lanes:
                finish(l, tb)

        border(4 + half)
        for l in lanes:
            finish(l, 0)

        @pl.loop(0, 32)
        def _(k):
            rows = pl.ds(pl.multiple_of(16 * k, 16), 16)
            for l in lanes:
                out_ref[rows, pl.ds(128 * l, 128)] = res[l, rows, :].astype(BF16)

    for p in range(len(PIECES)):
        gone = buf[p].at[pl.ds(0, 31)]
        remote(gone, gone, (q, c), zs.at[p], zr.at[p]).wait_send()
        remote(mid[p], mid[p], (q, c), p1s.at[p], p1r.at[p, 0]).wait_send()


def on_device(arrived, landing, resets, short_taps, decay_rate, residues, skip_gain):
    skip = jnp.broadcast_to(skip_gain.reshape(4, 1, 128), (4, 8, 128))
    vmem = pl.BlockSpec(memory_space=pltpu.VMEM)
    smem = pl.BlockSpec(memory_space=pltpu.SMEM)
    dma = pltpu.SemaphoreType.DMA
    widths = [128 * PARTS[half][1] for _, half in PIECES]
    return pl.pallas_call(
        kernel,
        out_shape=jax.ShapeDtypeStruct((512, 512), BF16),
        in_specs=[pl.BlockSpec(memory_space=pl.ANY), smem, smem, vmem, vmem, vmem, vmem],
        out_specs=vmem,
        scratch_shapes=[
            *[pltpu.VMEM((15, 32, w), BF16) for w in widths],
            *[pltpu.VMEM((32, 16, w), BF16) for w in widths],
            *[pltpu.VMEM((16, w), BF16) for w in widths],
            *[pltpu.VMEM((16, w), BF16) for w in widths],
            pltpu.VMEM((3, 4, 520, 128), F32),
            pltpu.VMEM((4, 64, 8, 128), F32),
            pltpu.VMEM((4, 64, 8, 128), F32),
            pltpu.VMEM((4, 512, 128), F32),
            pltpu.VMEM((64, 8, 128), F32),
            pltpu.VMEM((4, 16, 8, 128), F32),
            pltpu.VMEM((4, 16, 8, 128), F32),
            pltpu.VMEM((4, 16, 8, 128), F32),
            pltpu.VMEM((4, 16, 8, 128), F32),
            pltpu.VMEM((4, 16, 128), F32),
            pltpu.VMEM((16, 640), BF16),
            pltpu.VMEM((16, 640), BF16),
            pltpu.VMEM((4, 16, 640), BF16),
            pltpu.VMEM((4, 16, 640), BF16),
            pltpu.VMEM((3, 4, 16, 128), F32),
            pltpu.SMEM((32,), jnp.int32),
            dma((6,)), dma((6, 15)), dma((6,)), dma((6,)), dma((6,)), dma((6,)),
            dma, dma, dma, dma, dma, dma, pltpu.SemaphoreType.REGULAR,
        ],
        compiler_params=pltpu.CompilerParams(
            collective_id=0, has_side_effects=True, vmem_limit_bytes=40 << 20
        ),
        cost_estimate=pl.CostEstimate(flops=64 << 20, bytes_accessed=4 << 20, transcendentals=1 << 15),
    )(arrived, landing, resets, short_taps, decay_rate, residues, skip)


def solution(mesh):
    in_specs = (
        P(None, ("seq", "chan"), None),
        P("seq", None),
        P("seq"),
        P(None, None, "chan"),
        P(None, "chan"),
        P(None, "chan"),
        P("chan"),
    )
    return jax.shard_map(
        on_device, mesh=mesh, in_specs=in_specs, out_specs=P("seq", "chan"), check_vma=False
    )
```

```python
import jax
import jax.numpy as jnp
from jax import lax
from jax.experimental import pallas as pl
from jax.experimental.pallas import tpu as pltpu
from jax.sharding import PartitionSpec as P

MESH = pl.DeviceIdType.MESH
PARTS = ((0, 2), (2, 2))
PIECES = ((1, 0), (2, 0), (1, 1), (2, 1), (0, 0), (0, 1))
UNROLL = 8
F32 = jnp.float32
BF16 = jnp.bfloat16


def one_minus_exp(u):
    series = jnp.ones_like(u)
    for k in range(10, 1, -1):
        series = 1.0 - (u * (1.0 / k)) * series
    return jnp.where(u < 0.5, u * series, 1.0 - jnp.exp(-u))


def kernel(
    a_ref, land_ref, reset_ref, taps_ref, rate_ref, resid_ref, skip_ref, out_ref,
    mid0, mid1, mid2, mid3, mid4, mid5, buf0, buf1, buf2, buf3, buf4, buf5,
    hsend0, hsend1, hsend2, hsend3, hsend4, hsend5, hrecv0, hrecv1, hrecv2, hrecv3, hrecv4, hrecv5, ext, gated, modal, res, keep, step_decay, weight, enter, through,
    ends, msg0, sib, l1buf, l2buf, entering, src,
    p1s, p1r, zs, zr, hs, hr, l0s, l0r, l1s, l1r, l2s, l2r, far,
):
    q = lax.axis_index("seq")
    c = lax.axis_index("chan")
    z = q // 2
    core = q % 2
    group, member = z // 4, z % 4

    def remote(source, target, device, send, recv):
        return pltpu.make_async_remote_copy(
            src_ref=source, dst_ref=target, send_sem=send, recv_sem=recv,
            device_id=device, device_id_type=MESH,
        )

    barrier = pltpu.get_barrier_semaphore()

    def greet(device):
        pl.semaphore_signal(barrier, inc=1, device_id=device, device_id_type=MESH)

    @pl.loop(1, 16)
    def _(i):
        greet((q, lax.rem(c + i, 16)))

    @pl.loop(1, 5)
    def _(i):
        for k in range(2):
            greet((2 * lax.rem(z + i, 16) + k, c))
            greet((2 * lax.rem(z + 16 - i, 16) + k, c))

    greet((q + 1 - 2 * core, c))
    pl.semaphore_wait(barrier, 32)
    for beyond in (8, 24):
        pl.semaphore_signal(far, inc=1, device_id=(lax.rem(q + beyond, 32), c), device_id_type=MESH)

    mid = (mid0, mid1, mid2, mid3, mid4, mid5)
    buf = (buf0, buf1, buf2, buf3, buf4, buf5)
    hsend = (hsend0, hsend1, hsend2, hsend3, hsend4, hsend5)
    hrecv = (hrecv0, hrecv1, hrecv2, hrecv3, hrecv4, hrecv5)

    def columns(dc, half):
        group0, groups = PARTS[half]
        return pl.ds(pl.multiple_of(dc * 512 + 128 * group0, 128), 128 * groups)

    def shift_at(j):
        return lax.rem(j - 1 + z, 15) + 1

    def plane_send(p, j):
        f, half = PIECES[p]
        dc = lax.rem(c + 16 - shift_at(j), 16)
        remote(a_ref.at[f, :, columns(dc, half)], mid[p].at[j - 1], (q, dc), p1s.at[p], p1r.at[p, j - 1]).start()

    def ring_send(p, block, target_z):
        for k in range(2):
            to = 2 * target_z + k
            rows = block.at[pl.ds(16 * k, 16)]

            @pl.when(to == q)
            def _():
                pltpu.make_async_copy(rows, buf[p].at[q], zr.at[p]).start()

            @pl.when(to != q)
            def _():
                remote(rows, buf[p].at[q], (to, c), zs.at[p], zr.at[p]).start()

    def forward_far_first(p, first, stop):
        f, half = PIECES[p]

        @pl.loop(first, stop)
        def _(i):
            reach = 8 - (i + 1) // 2
            target = lax.rem(z + 16 + reach * (2 * lax.rem(i, 2) - 1), 16)
            shift = lax.rem(target + 16 - c, 16)
            j = lax.rem(shift + 29 - z, 15) + 1

            @pl.when(shift == 0)
            def _():
                ring_send(p, a_ref.at[f, :, columns(c, half)], target)

            @pl.when(shift != 0)
            def _():
                remote(mid[p].at[j - 1], mid[p].at[j - 1], (q, c), p1s.at[p], p1r.at[p, j - 1]).wait_recv()
                ring_send(p, mid[p].at[j - 1], target)

    def forward(p, first=0, stop=16):
        f, half = PIECES[p]
        if first == 0:
            ring_send(p, a_ref.at[f, :, columns(c, half)], c)

        @pl.loop(max(first, 1), stop)
        def _(j):
            remote(mid[p].at[j - 1], mid[p].at[j - 1], (q, c), p1s.at[p], p1r.at[p, j - 1]).wait_recv()
            ring_send(p, mid[p].at[j - 1], lax.rem(c + shift_at(j), 16))
            for ahead in ((p + 1,) if p < 3 else (4, 5) if p == 3 else ()):
                plane_send(ahead, j)

    @pl.loop(1, 16)
    def _(j):
        plane_send(0, j)

    @pl.loop(0, 32)
    def _(k):
        total = jnp.int32(0)
        for s in range(32):
            total = jnp.where(land_ref[0, s] == k, jnp.int32(s), total)
        src[k] = total

    pl.semaphore_wait(far, 2)
    forward(0)

    sub = lax.broadcasted_iota(jnp.int32, (8, 128), 0)

    @pl.loop(0, 64)
    def _(t):
        marks = jnp.zeros((8, 128), jnp.int32)
        for i in range(8):
            marks = jnp.where(sub == i, reset_ref[64 * i + t], marks)
        keep[t] = (1 - marks).astype(F32)

    for l in range(4):
        lanes = pl.ds(128 * l, 128)
        rate = rate_ref[:, lanes]
        decay = jnp.exp(-rate)
        gain = resid_ref[:, lanes] * jnp.sqrt(one_minus_exp(2.0 * rate))
        step_decay[l] = jnp.broadcast_to(decay[:, None, :], (16, 8, 128))
        weight[l] = jnp.broadcast_to(gain[:, None, :], (16, 8, 128))

    kept = lax.fori_loop(0, 64, lambda t, v: v * keep[t], jnp.ones((8, 128), F32))

    for p in (1, 2, 3):
        forward(p)

    def sum16(v):
        v = v[:8] + v[8:]
        v = v[:4] + v[4:]
        v = v[:2] + v[2:]
        return v[0] + v[1]

    def arrived_piece(p):
        f, half = PIECES[p]
        remote(buf[p], buf[p], (q, c), zs.at[p], zr.at[p]).wait_recv()
        hsend[p][...] = buf[p][src[31]]
        remote(hsend[p], hrecv[p], (lax.rem(q + 1, 32), c), hs.at[p], hr.at[p]).start()

        @pl.loop(0, 32)
        def _(k):
            at_row = pl.multiple_of(8 + 16 * k, 8)
            for i in range(PARTS[half][1]):
                ext[f, PARTS[half][0] + i, pl.ds(at_row, 16), :] = buf[p][src[k], :, pl.ds(128 * i, 128)].astype(F32)

    def border(p):
        f, half = PIECES[p]
        remote(hsend[p], hrecv[p], (q, c), hs.at[p], hr.at[p]).wait()
        for i in range(PARTS[half][1]):
            tail = hrecv[p][:, pl.ds(128 * i, 128)].astype(F32)[8:16]
            ext[f, PARTS[half][0] + i, pl.ds(0, 8), :] = jnp.where(q == 0, jnp.zeros_like(tail), tail)

    def conv(f, l, tb):
        first_row = 2 + 8 * tb
        window = jnp.stack([ext[f, l, pl.ds(first_row + m, 8, stride=64), :] for m in range(14)])
        total = taps_ref[f, pl.ds(0, 1), pl.ds(128 * l, 128)][None] * window[6:14]
        for j in range(1, 7):
            total = total + taps_ref[f, pl.ds(j, 1), pl.ds(128 * l, 128)][None] * window[6 - j : 14 - j]
        return total

    def gate(l, tb):
        product = conv(1, l, tb) * conv(2, l, tb)
        gated[l, pl.ds(8 * tb, 8)] = product.astype(BF16).astype(F32)

    def scan_lanes(l):
        skip = skip_ref[l]

        def advance(step, states):
            for u in range(UNROLL):
                t = UNROLL * step + u
                value = gated[l, t]
                states = states * (step_decay[l] * keep[t][None]) + value[None]
                modal[l, t] = skip * value + sum16(weight[l] * states)
            return states

        states = lax.fori_loop(0, 64 // UNROLL, advance, jnp.zeros((16, 8, 128), F32))
        power = step_decay[l]
        for _ in range(6):
            power = power * power
        for n in range(16):
            a, b = power[n] * kept, states[n]
            for by in (1, 2, 4):
                a_before = jnp.where(sub < by, 1.0, pltpu.roll(a, by, 0))
                b_before = jnp.where(sub < by, 0.0, pltpu.roll(b, by, 0))
                b = b + a * b_before
                a = a * a_before
            ends[l, pl.ds(n, 1), :] = b[7:8]
            enter[l, n] = jnp.where(sub < 1, 0.0, pltpu.roll(b, 1, 0))
            through[l, n] = jnp.where(sub < 1, 1.0, pltpu.roll(a, 1, 0))

    def gate_and_scan(half):
        lanes = tuple(range(PARTS[half][0], sum(PARTS[half])))

        @pl.loop(1, 8)
        def _(tb):
            for l in lanes:
                gate(l, tb)

        border(2 * half)
        border(2 * half + 1)
        for l in lanes:
            gate(l, 0)
        pl.loop(lanes[0], lanes[-1] + 1)(scan_lanes)

    arrived_piece(0)
    arrived_piece(1)
    gate_and_scan(0)
    forward(4, 0, 6)
    arrived_piece(2)
    arrived_piece(3)
    forward(4, 6, 16)
    gate_and_scan(1)

    unbroken = kept
    for by in (4, 2, 1):
        unbroken = unbroken * pltpu.roll(unbroken, by, 0)
    whole_flag = jnp.concatenate([unbroken, unbroken], axis=0)

    for l in range(4):
        msg0[:, pl.ds(128 * l, 128)] = ends[l].astype(BF16)
    msg0[:, pl.ds(512, 128)] = whole_flag.astype(BF16)
    pair = remote(msg0, sib, (q + 1 - 2 * core, c), l0s, l0r)
    pair.start()
    pair.wait()
    flag_lanes = pl.ds(512, 128)
    own_flag = whole_flag
    sib_flag = sib[:, flag_lanes].astype(F32)
    low = core == 0
    flag0 = jnp.where(low, own_flag, sib_flag)
    flag1 = jnp.where(low, sib_flag, own_flag)

    def rates(l, count):
        return jnp.exp(rate_ref[:, pl.ds(128 * l, 128)] * (-float(count)))

    for l in range(4):
        lanes = pl.ds(128 * l, 128)
        own, other = ends[l], sib[:, lanes].astype(F32)
        end0, end1 = jnp.where(low, own, other), jnp.where(low, other, own)
        l1buf[member, :, lanes] = (end1 + rates(l, 512) * flag1 * end0).astype(BF16)
    l1buf[member, :, flag_lanes] = (flag0 * flag1).astype(BF16)

    for o in range(1, 4):
        to = 2 * (4 * group + lax.rem(member + o, 4)) + core
        remote(l1buf.at[member], l1buf.at[member], (to, c), l1s, l1r).start()
    forward_far_first(5, 0, 10)
    remote(l1buf.at[pl.ds(0, 3)], l1buf.at[pl.ds(0, 3)], (q, c), l1s, l1r).wait()

    def combine(table, mine, l, count):
        lanes = pl.ds(128 * l, 128)
        power = rates(l, count)
        total = jnp.zeros((16, 128), F32)
        before = jnp.zeros((16, 128), F32)
        passed = jnp.ones((16, 128), F32)
        for i in range(4):
            end = table[i, :, lanes].astype(F32)
            factor = power * table[i, :, flag_lanes].astype(F32)
            earlier = mine > i
            before = jnp.where(earlier, before * factor + end, before)
            passed = jnp.where(earlier, passed * factor, passed)
            total = total * factor + end
        return before, passed, total

    for l in range(4):
        before, passed, total = combine(l1buf, member, l, 1024)
        l2buf[group, :, pl.ds(128 * l, 128)] = total.astype(BF16)
        ends_at = before
        entering[0, l] = ends_at
        entering[1, l] = passed
    flags = l1buf[0, :, flag_lanes] * l1buf[1, :, flag_lanes] * l1buf[2, :, flag_lanes] * l1buf[3, :, flag_lanes]
    l2buf[group, :, flag_lanes] = flags

    for o in range(1, 4):
        to = 2 * (4 * lax.rem(group + o, 4) + member) + core
        remote(l2buf.at[group], l2buf.at[group], (to, c), l2s, l2r).start()
    forward_far_first(5, 10, 16)
    remote(l2buf.at[pl.ds(0, 3)], l2buf.at[pl.ds(0, 3)], (q, c), l2s, l2r).wait()

    for l in range(4):
        lanes = pl.ds(128 * l, 128)
        before, _, _ = combine(l2buf, group, l, 4096)
        into_chip = entering[0, l] + entering[1, l] * before
        after_core0 = sib[:, lanes].astype(F32) + rates(l, 512) * sib_flag * into_chip
        entering[2, l] = jnp.where(low, into_chip, after_core0)

    @pl.loop(0, 4)
    def _(l):
        into = entering[2, l][:, None, :]
        start = weight[l] * (enter[l] + through[l] * into)

        def carry_on(step, carried):
            states, held = carried
            for u in range(UNROLL):
                t = UNROLL * step + u
                held = held * keep[t]
                states = states * step_decay[l]
                modal[l, t] = modal[l, t] + held * sum16(states)
            return states, held

        lax.fori_loop(0, 64 // UNROLL, carry_on, (start, jnp.ones((8, 128), F32)))

    def finish(l, tb):
        mixed = conv(0, l, tb) * modal[l, pl.ds(8 * tb, 8)]
        for u in range(8):
            res[l, pl.ds(8 * tb + u, 8, stride=64), :] = mixed[u]

    for half in range(2):
        lanes = tuple(range(PARTS[half][0], sum(PARTS[half])))
        arrived_piece(4 + half)

        @pl.loop(1, 8)
        def _(tb):
            for l in lanes:
                finish(l, tb)

        border(4 + half)
        for l in lanes:
            finish(l, 0)

        @pl.loop(0, 32)
        def _(k):
            rows = pl.ds(pl.multiple_of(16 * k, 16), 16)
            for l in lanes:
                out_ref[rows, pl.ds(128 * l, 128)] = res[l, rows, :].astype(BF16)

    for p in range(len(PIECES)):
        gone = buf[p].at[pl.ds(0, 31)]
        remote(gone, gone, (q, c), zs.at[p], zr.at[p]).wait_send()
        remote(mid[p], mid[p], (q, c), p1s.at[p], p1r.at[p, 0]).wait_send()


def on_device(arrived, landing, resets, short_taps, decay_rate, residues, skip_gain):
    skip = jnp.broadcast_to(skip_gain.reshape(4, 1, 128), (4, 8, 128))
    vmem = pl.BlockSpec(memory_space=pltpu.VMEM)
    smem = pl.BlockSpec(memory_space=pltpu.SMEM)
    dma = pltpu.SemaphoreType.DMA
    widths = [128 * PARTS[half][1] for _, half in PIECES]
    return pl.pallas_call(
        kernel,
        out_shape=jax.ShapeDtypeStruct((512, 512), BF16),
        in_specs=[pl.BlockSpec(memory_space=pl.ANY), smem, smem, vmem, vmem, vmem, vmem],
        out_specs=vmem,
        scratch_shapes=[
            *[pltpu.VMEM((15, 32, w), BF16) for w in widths],
            *[pltpu.VMEM((32, 16, w), BF16) for w in widths],
            *[pltpu.VMEM((16, w), BF16) for w in widths],
            *[pltpu.VMEM((16, w), BF16) for w in widths],
            pltpu.VMEM((3, 4, 520, 128), F32),
            pltpu.VMEM((4, 64, 8, 128), F32),
            pltpu.VMEM((4, 64, 8, 128), F32),
            pltpu.VMEM((4, 512, 128), F32),
            pltpu.VMEM((64, 8, 128), F32),
            pltpu.VMEM((4, 16, 8, 128), F32),
            pltpu.VMEM((4, 16, 8, 128), F32),
            pltpu.VMEM((4, 16, 8, 128), F32),
            pltpu.VMEM((4, 16, 8, 128), F32),
            pltpu.VMEM((4, 16, 128), F32),
            pltpu.VMEM((16, 640), BF16),
            pltpu.VMEM((16, 640), BF16),
            pltpu.VMEM((4, 16, 640), BF16),
            pltpu.VMEM((4, 16, 640), BF16),
            pltpu.VMEM((3, 4, 16, 128), F32),
            pltpu.SMEM((32,), jnp.int32),
            dma((6,)), dma((6, 15)), dma((6,)), dma((6,)), dma((6,)), dma((6,)),
            dma, dma, dma, dma, dma, dma, pltpu.SemaphoreType.REGULAR,
        ],
        compiler_params=pltpu.CompilerParams(
            collective_id=0, has_side_effects=True, vmem_limit_bytes=40 << 20
        ),
        cost_estimate=pl.CostEstimate(flops=64 << 20, bytes_accessed=4 << 20, transcendentals=1 << 15),
    )(arrived, landing, resets, short_taps, decay_rate, residues, skip)


def solution(mesh):
    in_specs = (
        P(None, ("seq", "chan"), None),
        P("seq", None),
        P("seq"),
        P(None, None, "chan"),
        P(None, "chan"),
        P(None, "chan"),
        P("chan"),
    )
    return jax.shard_map(
        on_device, mesh=mesh, in_specs=in_specs, out_specs=P("seq", "chan"), check_vma=False
    )
```
